128 devices in a mesh: fsdp: 16 (over y_hi, x, core), tp: 8 (over z, y_lo).
Axes of the slice: x: 4, y: 4 (y_hi: 2, y_lo: 2; y = y_hi * 2 + y_lo), z: 4, core: 2. Of those that a mesh axis runs over, the one named last changes fastest.
Arguments:
- hidden: bfloat16 [32768, 29568], P('fsdp', 'tp'), may hold values from -6 to 6
- out_grad: bfloat16 [32768, 8192], P('fsdp', 'tp'), may hold values from -0.03125 to 0.03125
- projector_bank: bfloat16 [16, 8192, 256], P('fsdp', 'tp'), may hold values from -0.0625 to 0.0625
- owner: int32 [1], replicated, may hold values from 0 to 15
- first_moment: float32 [8, 3696, 256], P('tp', 'fsdp'), may hold values from -4 to 4
- second_moment: float32 [8, 3696, 256], P('tp', 'fsdp'), may hold values from 0.05 to 2
Outputs:
- new_first: float32 [8, 3696, 256], P('tp', 'fsdp')
- new_second: float32 [8, 3696, 256], P('tp', 'fsdp')
- weight_update: bfloat16 [8, 3696, 8192], P('tp', 'fsdp')
The draws below stay inside these ranges and needn't reach their ends.
All inputs are finite; a program needn't handle non-finite values.
Results may differ from the reference program's by a relative error of at most 0.0051.
Values may be sent and summed in bfloat16 or wider, within the bound.
No kernel may reach another device: no remote copies, remote signals or barrier semaphores. Data moves between devices by JAX's collectives and lax.ppermute only.
A program may use at most 192 MiB of HBM per device.

```python
import math
import jax
import jax.numpy as jnp
from jax import lax

D = 8192
FF = 29568
RANK = 256
TOKENS = 32768
FF_TP = 3696
N_FSDP = 16
N_TP = 8


def block_scale(stream_key, extent, shards, least, high):
    def one(position, shards_of):
        draws = jax.random.uniform(jax.random.fold_in(jax.random.fold_in(stream_key, 6), position), (shards_of,), jnp.float32, least / len(shards), high / len(shards))
        return jnp.repeat(jnp.exp(draws), extent[position] // shards_of).reshape((-1,) + (1,) * (len(extent) - position - 1))

    level = one(*shards[0])
    for cut in shards[1:]:
        level = level * one(*cut)
    return level


def gaussian(key, shape, scale, bound, cuts=(), held_as=jnp.bfloat16):
    result = scale * jax.random.normal(key, shape, jnp.float32)
    if cuts:
        result = result * block_scale(key, shape, cuts, -0.22, 0.18)
    return jnp.clip(result, -bound, bound).astype(held_as)


def setup_inputs(seed: int = 0) -> dict:
    key_of = jax.random.split(jax.random.key(seed), 7)
    return {
        "hidden": gaussian(key_of[0], (TOKENS, FF), 1.0, 6.0, ((0, 16), (1, 8))),
        "out_grad": gaussian(key_of[1], (TOKENS, D), TOKENS ** -0.5, 0.03125, ((0, 16), (1, 8))),
        "projector_bank": gaussian(key_of[2], (N_FSDP, D, RANK), D ** -0.5, 0.0625, ((0, 16), (1, 8))),
        "owner": jax.random.randint(key_of[3], (1,), 0, N_FSDP).astype(jnp.int32),
        "first_moment": gaussian(key_of[4], (N_TP, FF_TP, RANK), 0.5, 4.0, ((0, 8), (1, 16)), jnp.float32),
        "second_moment": jnp.clip(jnp.exp(math.log(2.0) - 3.6888794 * jax.random.uniform(key_of[5], (N_TP, FF_TP, RANK), jnp.float32) ** block_scale(key_of[5], (N_TP, FF_TP, RANK), ((0, 8), (1, 16)), -0.2, 0.2)), 0.05, 2.0),
    }


def reference(hidden, out_grad, projector_bank, owner, first_moment, second_moment):
    projector = lax.dynamic_index_in_dim(projector_bank, owner[0].astype(jnp.int32), 0, keepdims=False)
    coeffs = jnp.dot(out_grad, projector, preferred_element_type=jnp.float32).astype(jnp.bfloat16)
    proj_grad = lax.dot_general(hidden, coeffs, (((0,), (0,)), ((), ())), preferred_element_type=jnp.float32)
    first = first_moment.reshape(FF, RANK)
    second = second_moment.reshape(FF, RANK)
    new_first = 0.9 * first + 0.1 * proj_grad
    new_second = 0.95 * second + 0.05 * proj_grad * proj_grad
    direction = (new_first / (jnp.sqrt(new_second) + 1e-08)).astype(jnp.bfloat16)
    update = lax.dot_general(direction, projector, (((1,), (1,)), ((), ())), preferred_element_type=jnp.float32)
    update = (-4.0 * update).astype(jnp.bfloat16)
    return (new_first.reshape(N_TP, FF // N_TP, RANK), new_second.reshape(N_TP, FF // N_TP, RANK), update.reshape(N_TP, FF // N_TP, D))
```

```python
import jax
import jax.numpy as jnp
from jax import lax
from jax.sharding import PartitionSpec as P

FSDP = ("yh", "x", "core")
CHIPS = ("yh", "x")
TP = ("z", "yl")
ROWS = 231
WIDE = 240


def starts(blocks, total):
    return [min(ROWS * i // 8 * 8, total - WIDE) for i in range(blocks)]


def local(hidden, out_grad, projector_bank, owner, first_moment, second_moment):
    bf16, f32 = jnp.bfloat16, jnp.float32
    root = owner[0]
    fsdp = lax.axis_index(FSDP)
    core = lax.axis_index("core")

    candidates = lax.all_to_all(projector_bank[0].reshape(16, 64, 256), FSDP, 0, 0)
    piece = lax.dynamic_index_in_dim(candidates, root, 0, keepdims=False)
    own_piece = lax.all_gather(piece, FSDP, axis=0, tiled=True)
    projector = lax.all_gather(own_piece, TP, axis=0, tiled=True)

    partial = jnp.dot(out_grad, own_piece, preferred_element_type=f32).astype(bf16)
    parts = lax.all_to_all(partial.reshape(8, 256, 256), TP, 0, 0)
    summed = jnp.sum(parts.astype(f32), axis=0).astype(bf16)
    coeffs = lax.all_to_all(
        jnp.broadcast_to(summed[None], (8, 256, 256)), TP, 0, 0
    ).reshape(2048, 256)

    grad = lax.dot_general(
        hidden, coeffs, (((0,), (0,)), ((), ())), preferred_element_type=f32
    )
    begin = starts(16, grad.shape[0])
    blocks = [grad[a : a + WIDE] for a in begin]
    even, odd = jnp.stack(blocks[0::2]), jnp.stack(blocks[1::2])
    keep = jnp.where(core == 0, even, odd)
    give = jnp.where(core == 0, odd, even).astype(bf16)
    got = lax.ppermute(give, "core", [(0, 1), (1, 0)])
    pair = (keep + got.astype(f32)).astype(bf16)
    shares = lax.all_to_all(pair, CHIPS, 0, 0)
    wide = jnp.sum(shares.astype(f32), axis=0)
    offset = ROWS * fsdp - jnp.array(begin, jnp.int32)[fsdp]
    proj_grad = lax.dynamic_slice_in_dim(wide, offset, ROWS, 0)

    new_first = 0.9 * first_moment[0] + 0.1 * proj_grad
    new_second = 0.95 * second_moment[0] + 0.05 * proj_grad * proj_grad
    direction = (new_first / (jnp.sqrt(new_second) + 1e-08)).astype(bf16)
    update = lax.dot_general(
        direction, projector, (((1,), (1,)), ((), ())), preferred_element_type=f32
    )
    update = (-4.0 * update).astype(bf16)
    return (new_first[None], new_second[None], update[None])


def solution(mesh):
    fine = jax.sharding.Mesh(
        mesh.devices.reshape(2, 4, 2, 4, 2), ("yh", "x", "core", "z", "yl")
    )
    in_specs = (
        P(FSDP, TP),
        P(FSDP, TP),
        P(FSDP, TP, None),
        P(),
        P(TP, FSDP, None),
        P(TP, FSDP, None),
    )
    out_specs = (P(TP, FSDP, None), P(TP, FSDP, None), P(TP, FSDP, None))
    return jax.shard_map(local, mesh=fine, in_specs=in_specs, out_specs=out_specs, check_vma=False)
```

```python
import jax
import jax.numpy as jnp
from jax import lax
from jax.experimental import pallas as pl
from jax.experimental.pallas import tpu as pltpu
from jax.sharding import PartitionSpec as P

FSDP = ("yh", "x", "core")
CHIPS = ("yh", "x")
TP = ("z", "yl")
ROWS = 231
PADDED = 232
BLOCK = 256
RANK = 256
bf16, f32 = jnp.bfloat16, jnp.float32


def cost(flops, moved):
    return pl.CostEstimate(flops=flops, bytes_accessed=moved, transcendentals=0)


def room(mebibytes):
    return pltpu.CompilerParams(vmem_limit_bytes=mebibytes << 20)


def stream(count, load, use):
    for i in range(3):
        load(i).start()

    @pl.loop(0, count)
    def _(i):
        load(i).wait()

        @pl.when(i + 3 < count)
        def _():
            load(i + 3).start()

        use(i)


def partial_kernel(where, mine, other, grad, out, piece, rows, done):
    core, share = where[0], where[1]
    half = mine.shape[0]

    def load(i):
        begin = 512 * i if isinstance(i, int) else pl.multiple_of(512 * i, 512)
        return pltpu.make_async_copy(grad.at[pl.ds(begin, 512)], rows.at[i], done.at[i])

    def use(i):
        product = jnp.dot(rows[i], piece[...], preferred_element_type=f32).astype(bf16)
        below = piece[pl.ds(pl.multiple_of(share * 128, 128), 128), :]
        for j in range(2):
            out[2 * i + j, :BLOCK, :] = product[BLOCK * j : BLOCK * (j + 1)]
            out[2 * i + j, BLOCK:, :] = below

    piece[pl.ds(pl.multiple_of(core * half, half), half), :] = mine[...]
    piece[pl.ds(pl.multiple_of((1 - core) * half, half), half), :] = other[...]
    stream(4, load, use)


def partial_and_share(where, mine, other, out_grad):
    vmem, any_space = pl.BlockSpec(memory_space=pltpu.VMEM), pl.BlockSpec(memory_space=pl.ANY)
    return pl.pallas_call(
        partial_kernel,
        in_specs=[pl.BlockSpec(memory_space=pltpu.SMEM), vmem, vmem, any_space],
        out_specs=vmem,
        out_shape=jax.ShapeDtypeStruct((8, BLOCK + 128, RANK), bf16),
        scratch_shapes=[
            pltpu.VMEM((1024, RANK), bf16),
            pltpu.VMEM((4, 512, 1024), bf16),
            pltpu.SemaphoreType.DMA((4,)),
        ],
        cost_estimate=cost(2 * 2048 * 1024 * 256, 6 << 20),
        compiler_params=room(59),
        name="partial_coeffs",
    )(where, mine, other, out_grad)


def sum_kernel(parts, out):
    total = parts[0].astype(f32)
    for i in range(1, 8):
        total += parts[i].astype(f32)
    total = total.astype(bf16)
    for i in range(8):
        out[i] = total


def sum_and_copies(parts):
    return pl.pallas_call(
        sum_kernel,
        grid=(1,),
        in_specs=[pl.BlockSpec((8, BLOCK, RANK), lambda i: (0, 0, 0))],
        out_specs=pl.BlockSpec((8, BLOCK, RANK), lambda i: (0, 0, 0)),
        out_shape=jax.ShapeDtypeStruct((8, BLOCK, RANK), bf16),
        cost_estimate=cost(8 * 65536, 2 << 20),
        compiler_params=room(8),
        name="sum_coeffs",
    )(parts)


def block_start(f):
    return jnp.minimum(ROWS * f // 16 * 16, 16 * ROWS - BLOCK)


def grad_kernel(parity, hidden, coeffs, out, rows, done):
    def load(i):
        begin = pl.multiple_of(block_start(2 * i + parity[0]), 16)
        return pltpu.make_async_copy(hidden.at[pl.ds(begin, BLOCK)], rows.at[i], done.at[i])

    def use(i):
        f = 2 * i + parity[0]
        block = jnp.dot(rows[i], coeffs[...], preferred_element_type=f32)
        block = pltpu.roll(block, BLOCK - (ROWS * f - block_start(f)), 0)
        out[i] = block[:PADDED].astype(out.dtype)

    stream(8, load, use)


def grad_blocks(parity, hidden_t, coeffs, dtype):
    return pl.pallas_call(
        grad_kernel,
        in_specs=[
            pl.BlockSpec(memory_space=pltpu.SMEM),
            pl.BlockSpec(memory_space=pl.ANY),
            pl.BlockSpec(memory_space=pltpu.VMEM),
        ],
        out_specs=pl.BlockSpec(memory_space=pltpu.VMEM),
        out_shape=jax.ShapeDtypeStruct((8, PADDED, RANK), dtype),
        scratch_shapes=[
            pltpu.VMEM((8, BLOCK, 2048), bf16),
            pltpu.SemaphoreType.DMA((8,)),
        ],
        cost_estimate=cost(2 * 2048 * 2048 * 256, 9 << 20),
        compiler_params=room(48),
        name="grad_blocks",
    )(parity, hidden_t, coeffs)


def final_kernel(
    shares, first, second, projector, new_first, new_second, update, direction, rows, blocks, came, left
):
    def load(i):
        return pltpu.make_async_copy(projector.at[:, i], rows.at[i], came.at[i])

    def store(i):
        begin = pl.multiple_of(1024 * i, 1024)
        return pltpu.make_async_copy(blocks.at[i], update.at[:, pl.ds(begin, 1024)], left.at[i])

    for i in range(8):
        load(i).start()
    grad = shares[0].astype(f32)
    for i in range(1, 8):
        grad += shares[i].astype(f32)
    grad = grad[:ROWS]
    moved = 0.9 * first[...] + 0.1 * grad
    scale = 0.95 * second[...] + 0.05 * grad * grad
    direction[...] = (moved / (jnp.sqrt(scale) + 1e-08)).astype(bf16)
    new_first[...] = moved.reshape(ROWS, 1, RANK)
    new_second[...] = scale.reshape(ROWS, 1, RANK)

    @pl.loop(0, 8)
    def _(i):
        load(i).wait()
        product = lax.dot_general(
            direction[...],
            rows[i].reshape(1024, RANK),
            (((1,), (1,)), ((), ())),
            preferred_element_type=f32,
        )
        blocks[i] = (-4.0 * product).astype(bf16)
        store(i).start()

    @pl.loop(0, 8)
    def _(i):
        store(i).wait()


def finish(shares, first, second, projector):
    vmem, any_space = pl.BlockSpec(memory_space=pltpu.VMEM), pl.BlockSpec(memory_space=pl.ANY)
    return pl.pallas_call(
        final_kernel,
        in_specs=[vmem, vmem, vmem, any_space],
        out_specs=[vmem, vmem, any_space],
        out_shape=[
            jax.ShapeDtypeStruct((ROWS, 1, RANK), f32),
            jax.ShapeDtypeStruct((ROWS, 1, RANK), f32),
            jax.ShapeDtypeStruct((ROWS, 8192), bf16),
        ],
        scratch_shapes=[
            pltpu.VMEM((ROWS, RANK), bf16),
            pltpu.VMEM((8, 8, 128, RANK), bf16),
            pltpu.VMEM((8, ROWS, 1024), bf16),
            pltpu.SemaphoreType.DMA((8,)),
            pltpu.SemaphoreType.DMA((8,)),
        ],
        cost_estimate=cost(2 * 231 * 8192 * 256, 10 << 20),
        compiler_params=room(56),
        name="adam_update",
    )(shares, first, second, projector)


def swap_cores(value):
    return lax.ppermute(value, FSDP, [(i, i ^ 1) for i in range(16)])


def shift(value, dx, dy):
    pairs = []
    for yh in range(2):
        for x in range(4):
            for core in range(2):
                to = ((yh + dy) % 2 * 4 + (x + dx) % 4) * 2 + core
                pairs.append(((yh * 4 + x) * 2 + core, to))
    return lax.ppermute(value, FSDP, pairs)


def owners_halves(candidate, root):
    yh, x, core = (lax.axis_index(a) for a in FSDP)
    halves = candidate.reshape(2, 512, RANK)
    kept = lax.dynamic_index_in_dim(halves, core, 0, keepdims=False)
    given = lax.dynamic_index_in_dim(halves, 1 - core, 0, keepdims=False)
    held = jnp.where(root % 2 == core, kept, swap_cores(given))
    dx = (x - root // 2 % 4) % 4
    dy = (yh - root // 8) % 2
    right, left, across = shift(held, 1, 0), shift(held, 3, 0), shift(held, 0, 1)
    held = jnp.where(
        (dx == 1) & (dy == 0),
        right,
        jnp.where((dx == 3) & (dy == 0), left, jnp.where((dx == 0) & (dy == 1), across, held)),
    )
    far, across = shift(held, 2, 0), shift(held, 0, 1)
    held = jnp.where(dx == 2, far, jnp.where((dx % 2 == 1) & (dy == 1), across, held))
    return held, swap_cores(held)


def local(hidden, out_grad, projector_bank, owner, first_moment, second_moment):
    core = lax.axis_index("core")
    column = lax.axis_index("x")

    mine, other = owners_halves(projector_bank[0], owner[0])
    where = jnp.stack([core, column * 2 + core]).astype(jnp.int32)
    hidden_t = hidden.T
    outgoing = partial_and_share(where, mine, other, out_grad)
    parts = lax.all_to_all(outgoing, TP, 0, 0)
    projector = lax.all_gather(parts[:, BLOCK:], ("x", "core"))
    coeffs = lax.all_to_all(sum_and_copies(parts), TP, 0, 0).reshape(2048, RANK)

    give = grad_blocks((1 - core)[None], hidden_t, coeffs, bf16)
    got = swap_cores(give)
    keep = grad_blocks(core[None], hidden_t, coeffs, f32)
    pair = (keep + got.astype(f32)).astype(bf16)
    shares = lax.all_to_all(pair, CHIPS, 0, 0)
    new_first, new_second, update = finish(shares, first_moment[0], second_moment[0], projector)
    return (new_first.transpose(1, 0, 2), new_second.transpose(1, 0, 2), update[None])


def solution(mesh):
    fine = jax.sharding.Mesh(
        mesh.devices.reshape(2, 4, 2, 4, 2), ("yh", "x", "core", "z", "yl")
    )
    in_specs = (
        P(FSDP, TP),
        P(FSDP, TP),
        P(FSDP, TP, None),
        P(),
        P(TP, FSDP, None),
        P(TP, FSDP, None),
    )
    out_specs = (P(TP, FSDP, None), P(TP, FSDP, None), P(TP, FSDP, None))
    return jax.shard_map(local, mesh=fine, in_specs=in_specs, out_specs=out_specs, check_vma=False)
```

```python
import jax
import jax.numpy as jnp
from jax import lax
from jax.experimental import pallas as pl
from jax.experimental.pallas import tpu as pltpu
from jax.sharding import PartitionSpec as P

FSDP = ("yh", "x", "core")
CHIPS = ("yh", "x")
TP = ("z", "yl")
ROWS = 231
PADDED = 232
BLOCK = 256
RANK = 256
bf16, f32 = jnp.bfloat16, jnp.float32


def cost(flops, moved):
    return pl.CostEstimate(flops=flops, bytes_accessed=moved, transcendentals=0)


def room(mebibytes):
    return pltpu.CompilerParams(vmem_limit_bytes=mebibytes << 20)


def partial_kernel(where, mine, other, grad, out, piece):
    core, half = where[0], mine.shape[0]
    piece[pl.ds(pl.multiple_of(core * half, half), half), :] = mine[...]
    piece[pl.ds(pl.multiple_of((1 - core) * half, half), half), :] = other[...]

    @pl.loop(0, 4)
    def _(i):
        rows = grad[pl.ds(pl.multiple_of(512 * i, 512), 512), :]
        product = jnp.dot(rows, piece[...], preferred_element_type=f32).astype(bf16)
        below = piece[pl.ds(pl.multiple_of(where[1] * 128, 128), 128), :]
        for j in range(2):
            out[2 * i + j, :BLOCK, :] = product[BLOCK * j : BLOCK * (j + 1)]
            out[2 * i + j, BLOCK:, :] = below


def partial_and_share(where, mine, other, out_grad):
    vmem = pl.BlockSpec(memory_space=pltpu.VMEM)
    return pl.pallas_call(
        partial_kernel,
        in_specs=[pl.BlockSpec(memory_space=pltpu.SMEM), vmem, vmem, vmem],
        out_specs=vmem,
        out_shape=jax.ShapeDtypeStruct((8, BLOCK + 128, RANK), bf16),
        scratch_shapes=[pltpu.VMEM((1024, RANK), bf16)],
        cost_estimate=cost(2 * 2048 * 1024 * 256, 6 << 20),
        compiler_params=room(12),
        name="partial_coeffs",
    )(where, mine, other, out_grad)


def sum_kernel(parts, out):
    total = parts[0].astype(f32)
    for i in range(1, 8):
        total += parts[i].astype(f32)
    total = total.astype(bf16)
    for i in range(8):
        out[i] = total


def sum_and_copies(parts):
    return pl.pallas_call(
        sum_kernel,
        grid=(1,),
        in_specs=[pl.BlockSpec((8, BLOCK, RANK), lambda i: (0, 0, 0))],
        out_specs=pl.BlockSpec((8, BLOCK, RANK), lambda i: (0, 0, 0)),
        out_shape=jax.ShapeDtypeStruct((8, BLOCK, RANK), bf16),
        cost_estimate=cost(8 * 65536, 2 << 20),
        compiler_params=room(8),
        name="sum_coeffs",
    )(parts)


def block_start(f):
    return jnp.minimum(ROWS * f // 16 * 16, 16 * ROWS - BLOCK)


def grad_kernel(parity, hidden, coeffs, out, rows, done):
    def load(i):
        begin = pl.multiple_of(block_start(2 * i + parity[0]), 16)
        return pltpu.make_async_copy(hidden.at[pl.ds(begin, BLOCK)], rows.at[i], done.at[i])

    for i in range(4):
        load(i).start()

    @pl.loop(0, 4)
    def _(pair):
        for j in range(2):
            load(2 * pair + j).wait()

        @pl.when(pair < 2)
        def _():
            for j in range(2):
                load(2 * pair + 4 + j).start()

        for j in range(2):
            i = 2 * pair + j
            f = 2 * i + parity[0]
            block = jnp.dot(rows[i], coeffs[...], preferred_element_type=f32)
            block = pltpu.roll(block, BLOCK - (ROWS * f - block_start(f)), 0)
            out[i] = block[:PADDED].astype(out.dtype)


def grad_blocks(parity, hidden_t, coeffs, dtype):
    return pl.pallas_call(
        grad_kernel,
        in_specs=[
            pl.BlockSpec(memory_space=pltpu.SMEM),
            pl.BlockSpec(memory_space=pl.ANY),
            pl.BlockSpec(memory_space=pltpu.VMEM),
        ],
        out_specs=pl.BlockSpec(memory_space=pltpu.VMEM),
        out_shape=jax.ShapeDtypeStruct((8, PADDED, RANK), dtype),
        scratch_shapes=[
            pltpu.VMEM((8, BLOCK, 2048), bf16),
            pltpu.SemaphoreType.DMA((8,)),
        ],
        cost_estimate=cost(2 * 2048 * 2048 * 256, 9 << 20),
        compiler_params=room(48),
        name="grad_blocks",
    )(parity, hidden_t, coeffs)


def final_kernel(
    shares, first, second, projector, new_first, new_second, update,
    parts, old, new, direction, rows, blocks, came, left,
):
    def load(i):
        return pltpu.make_async_copy(projector.at[:, i], rows.at[i], came.at[i])

    def store(i):
        begin = pl.multiple_of(1024 * i, 1024)
        return pltpu.make_async_copy(blocks.at[i], update.at[:, pl.ds(begin, 1024)], left.at[i])

    early = [
        pltpu.make_async_copy(shares, parts, came.at[8]),
        pltpu.make_async_copy(first, old.at[0], came.at[9]),
        pltpu.make_async_copy(second, old.at[1], came.at[10]),
    ]
    late = [
        pltpu.make_async_copy(new.at[0], new_first, left.at[8]),
        pltpu.make_async_copy(new.at[1], new_second, left.at[9]),
    ]
    for copy in early:
        copy.start()
    for i in range(8):
        load(i).start()
    for copy in early:
        copy.wait()
    grad = parts[0].astype(f32)
    for i in range(1, 8):
        grad += parts[i].astype(f32)
    grad = grad[:ROWS]
    moved = 0.9 * old[0].reshape(ROWS, RANK) + 0.1 * grad
    scale = 0.95 * old[1].reshape(ROWS, RANK) + 0.05 * grad * grad
    direction[...] = (moved / (jnp.sqrt(scale) + 1e-08)).astype(bf16)
    new[0] = moved.reshape(ROWS, 1, RANK)
    new[1] = scale.reshape(ROWS, 1, RANK)
    for copy in late:
        copy.start()

    @pl.loop(0, 8)
    def _(i):
        load(i).wait()
        product = lax.dot_general(
            direction[...],
            rows[i].reshape(1024, RANK),
            (((1,), (1,)), ((), ())),
            preferred_element_type=f32,
        )
        blocks[i] = (-4.0 * product).astype(bf16)
        store(i).start()

    @pl.loop(0, 8)
    def _(i):
        store(i).wait()

    for copy in late:
        copy.wait()


def finish(shares, first, second, projector):
    any_space = pl.BlockSpec(memory_space=pl.ANY)
    return pl.pallas_call(
        final_kernel,
        in_specs=[any_space] * 4,
        out_specs=[any_space] * 3,
        out_shape=[
            jax.ShapeDtypeStruct((ROWS, 1, RANK), f32),
            jax.ShapeDtypeStruct((ROWS, 1, RANK), f32),
            jax.ShapeDtypeStruct((ROWS, 8192), bf16),
        ],
        scratch_shapes=[
            pltpu.VMEM((8, PADDED, RANK), bf16),
            pltpu.VMEM((2, ROWS, 1, RANK), f32),
            pltpu.VMEM((2, ROWS, 1, RANK), f32),
            pltpu.VMEM((ROWS, RANK), bf16),
            pltpu.VMEM((8, 8, 128, RANK), bf16),
            pltpu.VMEM((8, ROWS, 1024), bf16),
            pltpu.SemaphoreType.DMA((11,)),
            pltpu.SemaphoreType.DMA((10,)),
        ],
        cost_estimate=cost(2 * 231 * 8192 * 256, 10 << 20),
        compiler_params=room(57),
        name="adam_update",
    )(shares, first, second, projector)


def swap_cores(value):
    return lax.ppermute(value, FSDP, [(i, i ^ 1) for i in range(16)])


def shift(value, dx, dy):
    pairs = []
    for yh in range(2):
        for x in range(4):
            for core in range(2):
                to = ((yh + dy) % 2 * 4 + (x + dx) % 4) * 2 + core
                pairs.append(((yh * 4 + x) * 2 + core, to))
    return lax.ppermute(value, FSDP, pairs)


def owners_halves(candidate, root):
    yh, x, core = (lax.axis_index(a) for a in FSDP)
    halves = candidate.reshape(2, 512, RANK)
    kept = lax.dynamic_index_in_dim(halves, core, 0, keepdims=False)
    given = lax.dynamic_index_in_dim(halves, 1 - core, 0, keepdims=False)
    held = jnp.where(root % 2 == core, kept, swap_cores(given))
    dx = (x - root // 2 % 4) % 4
    dy = (yh - root // 8) % 2
    right, left, across = shift(held, 1, 0), shift(held, 3, 0), shift(held, 0, 1)
    held = jnp.where(
        (dx == 1) & (dy == 0),
        right,
        jnp.where((dx == 3) & (dy == 0), left, jnp.where((dx == 0) & (dy == 1), across, held)),
    )
    far, across = shift(held, 2, 0), shift(held, 0, 1)
    held = jnp.where(dx == 2, far, jnp.where((dx % 2 == 1) & (dy == 1), across, held))
    return held, swap_cores(held)


def local(hidden, out_grad, projector_bank, owner, first_moment, second_moment):
    core = lax.axis_index("core")
    column = lax.axis_index("x")

    mine, other = owners_halves(projector_bank[0], owner[0])
    where = jnp.stack([core, column * 2 + core]).astype(jnp.int32)
    outgoing = partial_and_share(where, mine, other, out_grad)
    parts = lax.all_to_all(outgoing, TP, 0, 0)
    projector = lax.all_gather(parts[:, BLOCK:], ("x", "core"))
    coeffs = lax.all_to_all(sum_and_copies(parts), TP, 0, 0).reshape(2048, RANK)

    hidden_t = hidden.T
    give = grad_blocks((1 - core)[None], hidden_t, coeffs, bf16)
    got = swap_cores(give)
    keep = grad_blocks(core[None], hidden_t, coeffs, f32)
    pair = (keep + got.astype(f32)).astype(bf16)
    shares = lax.all_to_all(pair, CHIPS, 0, 0)
    new_first, new_second, update = finish(
        shares, first_moment.transpose(1, 0, 2), second_moment.transpose(1, 0, 2), projector
    )
    return (new_first.transpose(1, 0, 2), new_second.transpose(1, 0, 2), update[None])


def solution(mesh):
    fine = jax.sharding.Mesh(
        mesh.devices.reshape(2, 4, 2, 4, 2), ("yh", "x", "core", "z", "yl")
    )
    in_specs = (
        P(FSDP, TP),
        P(FSDP, TP),
        P(FSDP, TP, None),
        P(),
        P(TP, FSDP, None),
        P(TP, FSDP, None),
    )
    out_specs = (P(TP, FSDP, None), P(TP, FSDP, None), P(TP, FSDP, None))
    return jax.shard_map(local, mesh=fine, in_specs=in_specs, out_specs=out_specs, check_vma=False)
```

```python
import jax
import jax.numpy as jnp
from jax import lax
from jax.experimental import pallas as pl
from jax.experimental.pallas import tpu as pltpu
from jax.sharding import PartitionSpec as P

FSDP = ("yh", "x", "core")
CHIPS = ("yh", "x")
TP = ("z", "yl")
ROWS = 231
PADDED = 232
BLOCK = 256
RANK = 256
bf16, f32 = jnp.bfloat16, jnp.float32


def cost(flops, moved):
    return pl.CostEstimate(flops=flops, bytes_accessed=moved, transcendentals=0)


def room(mebibytes):
    return pltpu.CompilerParams(vmem_limit_bytes=mebibytes << 20)


def partial_kernel(where, mine, other, grad, out, piece):
    core, half = where[0], mine.shape[0]
    piece[pl.ds(pl.multiple_of(core * half, half), half), :] = mine[...]
    piece[pl.ds(pl.multiple_of((1 - core) * half, half), half), :] = other[...]

    @pl.loop(0, 4)
    def _(i):
        rows = grad[pl.ds(pl.multiple_of(512 * i, 512), 512), :]
        product = jnp.dot(rows, piece[...], preferred_element_type=f32).astype(bf16)
        below = piece[pl.ds(pl.multiple_of(where[1] * 128, 128), 128), :]
        for j in range(2):
            out[2 * i + j, :BLOCK, :] = product[BLOCK * j : BLOCK * (j + 1)]
            out[2 * i + j, BLOCK:, :] = below


def partial_and_share(where, mine, other, out_grad):
    vmem = pl.BlockSpec(memory_space=pltpu.VMEM)
    return pl.pallas_call(
        partial_kernel,
        in_specs=[pl.BlockSpec(memory_space=pltpu.SMEM), vmem, vmem, vmem],
        out_specs=vmem,
        out_shape=jax.ShapeDtypeStruct((8, BLOCK + 128, RANK), bf16),
        scratch_shapes=[pltpu.VMEM((1024, RANK), bf16)],
        cost_estimate=cost(2 * 2048 * 1024 * 256, 6 << 20),
        compiler_params=room(12),
        name="partial_coeffs",
    )(where, mine, other, out_grad)


def sum_kernel(parts, out):
    total = parts[0].astype(f32)
    for i in range(1, 8):
        total += parts[i].astype(f32)
    total = total.astype(bf16)
    for i in range(8):
        out[i] = total


def sum_and_copies(parts):
    return pl.pallas_call(
        sum_kernel,
        grid=(1,),
        in_specs=[pl.BlockSpec((8, BLOCK, RANK), lambda i: (0, 0, 0))],
        out_specs=pl.BlockSpec((8, BLOCK, RANK), lambda i: (0, 0, 0)),
        out_shape=jax.ShapeDtypeStruct((8, BLOCK, RANK), bf16),
        cost_estimate=cost(8 * 65536, 2 << 20),
        compiler_params=room(8),
        name="sum_coeffs",
    )(parts)


def block_start(f):
    return jnp.minimum(ROWS * f // 16 * 16, 16 * ROWS - BLOCK)


def grad_kernel(parity, hidden, coeffs, out, rows, done):
    def load(i):
        begin = pl.multiple_of(block_start(2 * i + parity[0]), 16)
        return pltpu.make_async_copy(hidden.at[pl.ds(begin, BLOCK)], rows.at[i], done.at[i])

    for i in range(4):
        load(i).start()

    @pl.loop(0, 4)
    def _(pair):
        for j in range(2):
            load(2 * pair + j).wait()

        @pl.when(pair < 2)
        def _():
            for j in range(2):
                load(2 * pair + 4 + j).start()

        for j in range(2):
            i = 2 * pair + j
            f = 2 * i + parity[0]
            block = jnp.dot(rows[i], coeffs[...], preferred_element_type=f32)
            block = pltpu.roll(block, BLOCK - (ROWS * f - block_start(f)), 0)
            out[i] = block[:PADDED].astype(out.dtype)


def grad_blocks(parity, hidden_t, coeffs, dtype):
    return pl.pallas_call(
        grad_kernel,
        in_specs=[
            pl.BlockSpec(memory_space=pltpu.SMEM),
            pl.BlockSpec(memory_space=pl.ANY),
            pl.BlockSpec(memory_space=pltpu.VMEM),
        ],
        out_specs=pl.BlockSpec(memory_space=pltpu.VMEM),
        out_shape=jax.ShapeDtypeStruct((8, PADDED, RANK), dtype),
        scratch_shapes=[
            pltpu.VMEM((8, BLOCK, 2048), bf16),
            pltpu.SemaphoreType.DMA((8,)),
        ],
        cost_estimate=cost(2 * 2048 * 2048 * 256, 9 << 20),
        compiler_params=room(48),
        name="grad_blocks",
    )(parity, hidden_t, coeffs)


def final_kernel(where, shares, first, second, *refs):
    pieces, (new_first, new_second, update) = refs[:10], refs[10:13]
    parts, old, new, direction, rows, blocks, came, left = refs[13:]
    column, core = where[0], where[1]

    def loads(half):
        copies = []
        for i in range(8):
            away, side = (0, 3, 1, 2)[i // 2], i % 2
            if away == 2:
                source = pieces[6 + 2 * half + side]
            else:
                source = pieces[i].at[pl.ds(4 * half, 4)]
            slot = 2 * ((column + away) % 4) + (core + side) % 2
            to = rows.at[pl.ds(4 * half, 4), slot]
            copies.append(pltpu.make_async_copy(source, to, came.at[8 * half + i]))
        return copies

    def store(i):
        begin = pl.multiple_of(1024 * i, 1024)
        return pltpu.make_async_copy(blocks.at[i], update.at[:, pl.ds(begin, 1024)], left.at[i])

    early = [
        pltpu.make_async_copy(shares, parts, came.at[16]),
        pltpu.make_async_copy(first, old.at[0], came.at[17]),
        pltpu.make_async_copy(second, old.at[1], came.at[18]),
    ]
    late = [
        pltpu.make_async_copy(new.at[0], new_first, left.at[8]),
        pltpu.make_async_copy(new.at[1], new_second, left.at[9]),
    ]
    for copy in early:
        copy.start()
    for half in range(2):
        for copy in loads(half):
            copy.start()
    for copy in early:
        copy.wait()
    grad = parts[0].astype(f32)
    for i in range(1, 8):
        grad += parts[i].astype(f32)
    grad = grad[:ROWS]
    moved = 0.9 * old[0].reshape(ROWS, RANK) + 0.1 * grad
    scale = 0.95 * old[1].reshape(ROWS, RANK) + 0.05 * grad * grad
    direction[...] = (moved / (jnp.sqrt(scale) + 1e-08)).astype(bf16)
    new[0] = moved.reshape(ROWS, 1, RANK)
    new[1] = scale.reshape(ROWS, 1, RANK)
    for copy in late:
        copy.start()
    for half in range(2):
        for copy in loads(half):
            copy.wait()

        @pl.loop(4 * half, 4 * half + 4)
        def _(i):
            product = lax.dot_general(
                direction[...],
                rows[i].reshape(1024, RANK),
                (((1,), (1,)), ((), ())),
                preferred_element_type=f32,
            )
            blocks[i] = (-4.0 * product).astype(bf16)
            store(i).start()

    @pl.loop(0, 8)
    def _(i):
        store(i).wait()

    for copy in late:
        copy.wait()


def finish(where, shares, first, second, pieces):
    any_space = pl.BlockSpec(memory_space=pl.ANY)
    return pl.pallas_call(
        final_kernel,
        in_specs=[pl.BlockSpec(memory_space=pltpu.SMEM)] + [any_space] * 13,
        out_specs=[any_space] * 3,
        out_shape=[
            jax.ShapeDtypeStruct((ROWS, 1, RANK), f32),
            jax.ShapeDtypeStruct((ROWS, 1, RANK), f32),
            jax.ShapeDtypeStruct((ROWS, 8192), bf16),
        ],
        scratch_shapes=[
            pltpu.VMEM((8, PADDED, RANK), bf16),
            pltpu.VMEM((2, ROWS, 1, RANK), f32),
            pltpu.VMEM((2, ROWS, 1, RANK), f32),
            pltpu.VMEM((ROWS, RANK), bf16),
            pltpu.VMEM((8, 8, 128, RANK), bf16),
            pltpu.VMEM((8, ROWS, 1024), bf16),
            pltpu.SemaphoreType.DMA((19,)),
            pltpu.SemaphoreType.DMA((10,)),
        ],
        cost_estimate=cost(2 * 231 * 8192 * 256, 10 << 20),
        compiler_params=room(57),
        name="adam_update",
    )(where, shares, first, second, *pieces)


def swap_cores(value):
    return lax.ppermute(value, FSDP, [(i, i ^ 1) for i in range(16)])


def shift(value, dx, dy):
    pairs = []
    for yh in range(2):
        for x in range(4):
            for core in range(2):
                to = ((yh + dy) % 2 * 4 + (x + dx) % 4) * 2 + core
                pairs.append(((yh * 4 + x) * 2 + core, to))
    return lax.ppermute(value, FSDP, pairs)


def owners_halves(candidate, root):
    yh, x, core = (lax.axis_index(a) for a in FSDP)
    halves = candidate.reshape(2, 512, RANK)
    kept = lax.dynamic_index_in_dim(halves, core, 0, keepdims=False)
    given = lax.dynamic_index_in_dim(halves, 1 - core, 0, keepdims=False)
    held = jnp.where(root % 2 == core, kept, swap_cores(given))
    dx = (x - root // 2 % 4) % 4
    dy = (yh - root // 8) % 2
    right, left, across = shift(held, 1, 0), shift(held, 3, 0), shift(held, 0, 1)
    held = jnp.where(
        (dx == 1) & (dy == 0),
        right,
        jnp.where((dx == 3) & (dy == 0), left, jnp.where((dx == 0) & (dy == 1), across, held)),
    )
    far, across = shift(held, 2, 0), shift(held, 0, 1)
    held = jnp.where(dx == 2, far, jnp.where((dx % 2 == 1) & (dy == 1), across, held))
    return held, swap_cores(held)


def local(hidden, out_grad, projector_bank, owner, first_moment, second_moment):
    core = lax.axis_index("core")
    column = lax.axis_index("x")

    mine, other = owners_halves(projector_bank[0], owner[0])
    where = jnp.stack([core, column * 2 + core]).astype(jnp.int32)
    outgoing = partial_and_share(where, mine, other, out_grad)
    parts = lax.all_to_all(outgoing, TP, 0, 0)
    share = parts[:, BLOCK:]
    coeffs = lax.all_to_all(sum_and_copies(parts), TP, 0, 0).reshape(2048, RANK)
    coeffs, left, right = lax.optimization_barrier(
        (coeffs, shift(share, 1, 0), shift(share, 3, 0))
    )
    ring = [share, left, right, shift(left[:4], 1, 0), shift(right[4:], 3, 0)]

    hidden_t = hidden.T
    give = grad_blocks((1 - core)[None], hidden_t, coeffs, bf16)
    got = swap_cores(give)
    keep = grad_blocks(core[None], hidden_t, coeffs, f32)
    pair = (keep + got.astype(f32)).astype(bf16)
    pair, *ring = lax.optimization_barrier((pair, *ring))
    shares = lax.all_to_all(pair, CHIPS, 0, 0)
    pieces = [side for piece in ring for side in (piece, swap_cores(piece))]
    new_first, new_second, update = finish(
        jnp.stack([column, core]).astype(jnp.int32),
        shares,
        first_moment.transpose(1, 0, 2),
        second_moment.transpose(1, 0, 2),
        pieces,
    )
    return (new_first.transpose(1, 0, 2), new_second.transpose(1, 0, 2), update[None])


def solution(mesh):
    fine = jax.sharding.Mesh(
        mesh.devices.reshape(2, 4, 2, 4, 2), ("yh", "x", "core", "z", "yl")
    )
    in_specs = (
        P(FSDP, TP),
        P(FSDP, TP),
        P(FSDP, TP, None),
        P(),
        P(TP, FSDP, None),
        P(TP, FSDP, None),
    )
    out_specs = (P(TP, FSDP, None), P(TP, FSDP, None), P(TP, FSDP, None))
    return jax.shard_map(local, mesh=fine, in_specs=in_specs, out_specs=out_specs, check_vma=False)
```

```python
import functools

import jax
import jax.numpy as jnp
from jax import lax
from jax.experimental import pallas as pl
from jax.experimental.pallas import tpu as pltpu
from jax.sharding import PartitionSpec as P

FSDP = ("yh", "x", "core")
CHIPS = ("yh", "x")
TP = ("z", "yl")
ROWS = 231
PADDED = 232
BLOCK = 256
RANK = 256
bf16, f32 = jnp.bfloat16, jnp.float32


def cost(flops, moved):
    return pl.CostEstimate(flops=flops, bytes_accessed=moved, transcendentals=0)


def room(mebibytes):
    return pltpu.CompilerParams(vmem_limit_bytes=mebibytes << 20)


def hold_kernel(count, source, out, done):
    rows = source.shape[0] // count
    copies = [
        pltpu.make_async_copy(
            source.at[pl.ds(rows * i, rows)], out.at[pl.ds(rows * i, rows)], done.at[i]
        )
        for i in range(count)
    ]
    for copy in copies:
        copy.start()
    for copy in copies:
        copy.wait()


def hold(source, count):
    return pl.pallas_call(
        functools.partial(hold_kernel, count),
        in_specs=[pl.BlockSpec(memory_space=pl.ANY)],
        out_specs=pl.BlockSpec(memory_space=pltpu.VMEM),
        out_shape=jax.ShapeDtypeStruct(source.shape, source.dtype),
        scratch_shapes=[pltpu.SemaphoreType.DMA((count,))],
        cost_estimate=cost(0, 4 * source.size),
        compiler_params=room(4),
        name="hold",
    )(source)


def partial_kernel(where, mine, other, grad, out, piece):
    core, half = where[0], mine.shape[0]
    piece[pl.ds(pl.multiple_of(core * half, half), half), :] = mine[...]
    piece[pl.ds(pl.multiple_of((1 - core) * half, half), half), :] = other[...]

    @pl.loop(0, 4)
    def _(i):
        rows = grad[pl.ds(pl.multiple_of(512 * i, 512), 512), :]
        product = jnp.dot(rows, piece[...], preferred_element_type=f32).astype(bf16)
        below = piece[pl.ds(pl.multiple_of(where[1] * 128, 128), 128), :]
        for j in range(2):
            out[2 * i + j, :BLOCK, :] = product[BLOCK * j : BLOCK * (j + 1)]
            out[2 * i + j, BLOCK:, :] = below


def partial_and_share(where, mine, other, out_grad):
    vmem = pl.BlockSpec(memory_space=pltpu.VMEM)
    return pl.pallas_call(
        partial_kernel,
        in_specs=[pl.BlockSpec(memory_space=pltpu.SMEM), vmem, vmem, vmem],
        out_specs=vmem,
        out_shape=jax.ShapeDtypeStruct((8, BLOCK + 128, RANK), bf16),
        scratch_shapes=[pltpu.VMEM((1024, RANK), bf16)],
        cost_estimate=cost(2 * 2048 * 1024 * 256, 6 << 20),
        compiler_params=room(12),
        name="partial_coeffs",
    )(where, mine, other, out_grad)


def sum_kernel(parts, out):
    total = parts[0].astype(f32)
    for i in range(1, 8):
        total += parts[i].astype(f32)
    total = total.astype(bf16)
    for i in range(8):
        out[i] = total


def sum_and_copies(parts):
    return pl.pallas_call(
        sum_kernel,
        grid=(1,),
        in_specs=[pl.BlockSpec((8, BLOCK, RANK), lambda i: (0, 0, 0))],
        out_specs=pl.BlockSpec((8, BLOCK, RANK), lambda i: (0, 0, 0)),
        out_shape=jax.ShapeDtypeStruct((8, BLOCK, RANK), bf16),
        cost_estimate=cost(8 * 65536, 2 << 20),
        compiler_params=room(8),
        name="sum_coeffs",
    )(parts)


def block_start(f):
    return jnp.minimum(ROWS * f // 16 * 16, 16 * ROWS - BLOCK)


def grad_kernel(parity, hidden, coeffs, out, rows, done):
    def load(i):
        begin = pl.multiple_of(block_start(2 * i + parity[0]), 16)
        return pltpu.make_async_copy(hidden.at[pl.ds(begin, BLOCK)], rows.at[i], done.at[i])

    for i in range(4):
        load(i).start()

    @pl.loop(0, 4)
    def _(pair):
        for j in range(2):
            load(2 * pair + j).wait()

        @pl.when(pair < 2)
        def _():
            for j in range(2):
                load(2 * pair + 4 + j).start()

        for j in range(2):
            i = 2 * pair + j
            f = 2 * i + parity[0]
            block = jnp.dot(rows[i], coeffs[...], preferred_element_type=f32)
            block = pltpu.roll(block, BLOCK - (ROWS * f - block_start(f)), 0)
            out[i] = block[:PADDED].astype(out.dtype)


def grad_blocks(parity, hidden_t, coeffs, dtype):
    return pl.pallas_call(
        grad_kernel,
        in_specs=[
            pl.BlockSpec(memory_space=pltpu.SMEM),
            pl.BlockSpec(memory_space=pl.ANY),
            pl.BlockSpec(memory_space=pltpu.VMEM),
        ],
        out_specs=pl.BlockSpec(memory_space=pltpu.VMEM),
        out_shape=jax.ShapeDtypeStruct((8, PADDED, RANK), dtype),
        scratch_shapes=[
            pltpu.VMEM((8, BLOCK, 2048), bf16),
            pltpu.SemaphoreType.DMA((8,)),
        ],
        cost_estimate=cost(2 * 2048 * 2048 * 256, 9 << 20),
        compiler_params=room(48),
        name="grad_blocks",
    )(parity, hidden_t, coeffs)


def final_kernel(where, shares, first, second, *refs):
    pieces, (new_first, new_second, update) = refs[:10], refs[10:13]
    parts, old, new, direction, rows, blocks, came, left = refs[13:]
    column, core = where[0], where[1]

    def loads(half):
        copies = []
        for i in range(8):
            away, side = (0, 3, 1, 2)[i // 2], i % 2
            if away == 2:
                source = pieces[6 + 2 * half + side]
            else:
                source = pieces[i].at[pl.ds(4 * half, 4)]
            slot = 2 * ((column + away) % 4) + (core + side) % 2
            to = rows.at[pl.ds(4 * half, 4), slot]
            copies.append(pltpu.make_async_copy(source, to, came.at[8 * half + i]))
        return copies

    def store(i):
        begin = pl.multiple_of(1024 * i, 1024)
        return pltpu.make_async_copy(blocks.at[i], update.at[:, pl.ds(begin, 1024)], left.at[i])

    early = [
        pltpu.make_async_copy(shares, parts, came.at[16]),
        pltpu.make_async_copy(first, old.at[0], came.at[17]),
        pltpu.make_async_copy(second, old.at[1], came.at[18]),
    ]
    late = [
        pltpu.make_async_copy(new.at[0], new_first, left.at[8]),
        pltpu.make_async_copy(new.at[1], new_second, left.at[9]),
    ]
    for copy in early:
        copy.start()
    for half in range(2):
        for copy in loads(half):
            copy.start()
    for copy in early:
        copy.wait()
    grad = parts[0].astype(f32)
    for i in range(1, 8):
        grad += parts[i].astype(f32)
    grad = grad[:ROWS]
    moved = 0.9 * old[0].reshape(ROWS, RANK) + 0.1 * grad
    scale = 0.95 * old[1].reshape(ROWS, RANK) + 0.05 * grad * grad
    direction[...] = (moved / (jnp.sqrt(scale) + 1e-08)).astype(bf16)
    new[0] = moved.reshape(ROWS, 1, RANK)
    new[1] = scale.reshape(ROWS, 1, RANK)
    for copy in late:
        copy.start()
    for half in range(2):
        for copy in loads(half):
            copy.wait()

        @pl.loop(4 * half, 4 * half + 4)
        def _(i):
            product = lax.dot_general(
                direction[...],
                rows[i].reshape(1024, RANK),
                (((1,), (1,)), ((), ())),
                preferred_element_type=f32,
            )
            blocks[i] = (-4.0 * product).astype(bf16)
            store(i).start()

    @pl.loop(0, 8)
    def _(i):
        store(i).wait()

    for copy in late:
        copy.wait()


def finish(where, shares, first, second, pieces):
    any_space = pl.BlockSpec(memory_space=pl.ANY)
    return pl.pallas_call(
        final_kernel,
        in_specs=[pl.BlockSpec(memory_space=pltpu.SMEM)] + [any_space] * 13,
        out_specs=[any_space] * 3,
        out_shape=[
            jax.ShapeDtypeStruct((ROWS, 1, RANK), f32),
            jax.ShapeDtypeStruct((ROWS, 1, RANK), f32),
            jax.ShapeDtypeStruct((ROWS, 8192), bf16),
        ],
        scratch_shapes=[
            pltpu.VMEM((8, PADDED, RANK), bf16),
            pltpu.VMEM((2, ROWS, 1, RANK), f32),
            pltpu.VMEM((2, ROWS, 1, RANK), f32),
            pltpu.VMEM((ROWS, RANK), bf16),
            pltpu.VMEM((8, 8, 128, RANK), bf16),
            pltpu.VMEM((8, ROWS, 1024), bf16),
            pltpu.SemaphoreType.DMA((19,)),
            pltpu.SemaphoreType.DMA((10,)),
        ],
        cost_estimate=cost(2 * 231 * 8192 * 256, 10 << 20),
        compiler_params=room(50),
        name="adam_update",
    )(where, shares, first, second, *pieces)


def swap_cores(value):
    return lax.ppermute(value, FSDP, [(i, i ^ 1) for i in range(16)])


def shift(value, dx, dy):
    pairs = []
    for yh in range(2):
        for x in range(4):
            for core in range(2):
                to = ((yh + dy) % 2 * 4 + (x + dx) % 4) * 2 + core
                pairs.append(((yh * 4 + x) * 2 + core, to))
    return lax.ppermute(value, FSDP, pairs)


def owners_halves(candidate, root, out_grad):
    yh, x, core = (lax.axis_index(a) for a in FSDP)
    halves = candidate.reshape(2, 512, RANK)
    kept = lax.dynamic_index_in_dim(halves, core, 0, keepdims=False)
    given = lax.dynamic_index_in_dim(halves, 1 - core, 0, keepdims=False)
    held = jnp.where(root % 2 == core, kept, swap_cores(given))
    dx = (x - root // 2 % 4) % 4
    dy = (yh - root // 8) % 2
    takes = [
        (dx == 1) & (dy == 0),
        (dx == 3) & (dy == 0),
        (dx == 0) & (dy == 1),
        dx == 2,
        (dx % 2 == 1) & (dy == 1),
    ]
    where = jnp.stack([core, x * 2 + core]).astype(jnp.int32)
    right, left, across = shift(held, 1, 0), shift(held, 3, 0), shift(held, 0, 1)
    out_grad, takes, where = lax.optimization_barrier((out_grad, takes, where))
    out_grad = hold(out_grad, 4)
    held = jnp.where(takes[0], right, jnp.where(takes[1], left, jnp.where(takes[2], across, held)))
    held, out_grad = lax.optimization_barrier((held, out_grad))
    far, across = shift(held, 2, 0), shift(held, 0, 1)
    held = jnp.where(takes[3], far, jnp.where(takes[4], across, held))
    return held, swap_cores(held), out_grad, where


def local(hidden, out_grad, projector_bank, owner, first_moment, second_moment):
    core = lax.axis_index("core")
    column = lax.axis_index("x")

    mine, other, held_grad, where = owners_halves(projector_bank[0], owner[0], out_grad)
    outgoing = partial_and_share(where, mine, other, held_grad)
    parts = lax.all_to_all(outgoing, TP, 0, 0)
    share = parts[:, BLOCK:]
    coeffs = lax.all_to_all(sum_and_copies(parts), TP, 0, 0).reshape(2048, RANK)

    hidden_t = hidden.T
    give = grad_blocks((1 - core)[None], hidden_t, coeffs, bf16)
    give, left, right = lax.optimization_barrier((give, shift(share, 1, 0), shift(share, 3, 0)))
    ring = [share, left, right, shift(left[:4], 1, 0), shift(right[4:], 3, 0)]
    got = swap_cores(give)
    keep = grad_blocks(core[None], hidden_t, coeffs, f32)
    pair = (keep + got.astype(f32)).astype(bf16)
    pair, *ring = lax.optimization_barrier((pair, *ring))
    shares = lax.all_to_all(pair, CHIPS, 0, 0)
    pieces = [side for piece in ring for side in (piece, swap_cores(piece))]
    new_first, new_second, update = finish(
        jnp.stack([column, core]).astype(jnp.int32),
        shares,
        first_moment.transpose(1, 0, 2),
        second_moment.transpose(1, 0, 2),
        pieces,
    )
    return (new_first.transpose(1, 0, 2), new_second.transpose(1, 0, 2), update[None])


def solution(mesh):
    fine = jax.sharding.Mesh(
        mesh.devices.reshape(2, 4, 2, 4, 2), ("yh", "x", "core", "z", "yl")
    )
    in_specs = (
        P(FSDP, TP),
        P(FSDP, TP),
        P(FSDP, TP, None),
        P(),
        P(TP, FSDP, None),
        P(TP, FSDP, None),
    )
    out_specs = (P(TP, FSDP, None), P(TP, FSDP, None), P(TP, FSDP, None))
    return jax.shard_map(local, mesh=fine, in_specs=in_specs, out_specs=out_specs, check_vma=False)
```

```python
import functools

import jax
import jax.numpy as jnp
from jax import lax
from jax.experimental import pallas as pl
from jax.experimental.pallas import tpu as pltpu
from jax.sharding import PartitionSpec as P

FSDP = ("yh", "x", "core")
CHIPS = ("yh", "x")
TP = ("z", "yl")
ROWS = 231
PADDED = 232
BLOCK = 256
RANK = 256
bf16, f32 = jnp.bfloat16, jnp.float32


def cost(flops, moved):
    return pl.CostEstimate(flops=flops, bytes_accessed=moved, transcendentals=0)


def room(mebibytes):
    return pltpu.CompilerParams(vmem_limit_bytes=mebibytes << 20)


def hold_kernel(count, source, out, done):
    rows = source.shape[0] // count
    copies = [
        pltpu.make_async_copy(
            source.at[pl.ds(rows * i, rows)], out.at[pl.ds(rows * i, rows)], done.at[i]
        )
        for i in range(count)
    ]
    for copy in copies:
        copy.start()
    for copy in copies:
        copy.wait()


def hold(source, count):
    return pl.pallas_call(
        functools.partial(hold_kernel, count),
        in_specs=[pl.BlockSpec(memory_space=pl.ANY)],
        out_specs=pl.BlockSpec(memory_space=pltpu.VMEM),
        out_shape=jax.ShapeDtypeStruct(source.shape, source.dtype),
        scratch_shapes=[pltpu.SemaphoreType.DMA((count,))],
        cost_estimate=cost(0, 4 * source.size),
        compiler_params=room(4),
        name="hold",
    )(source)


def partial_kernel(where, mine, other, grad, out, piece):
    core, half = where[0], mine.shape[0]
    piece[pl.ds(pl.multiple_of(core * half, half), half), :] = mine[...]
    piece[pl.ds(pl.multiple_of((1 - core) * half, half), half), :] = other[...]

    @pl.loop(0, 4)
    def _(i):
        rows = grad[pl.ds(pl.multiple_of(512 * i, 512), 512), :]
        product = jnp.dot(rows, piece[...], preferred_element_type=f32).astype(bf16)
        below = piece[pl.ds(pl.multiple_of(where[1] * 128, 128), 128), :]
        for j in range(2):
            out[2 * i + j, :BLOCK, :] = product[BLOCK * j : BLOCK * (j + 1)]
            out[2 * i + j, BLOCK:, :] = below


def partial_and_share(where, mine, other, out_grad):
    vmem = pl.BlockSpec(memory_space=pltpu.VMEM)
    return pl.pallas_call(
        partial_kernel,
        in_specs=[pl.BlockSpec(memory_space=pltpu.SMEM), vmem, vmem, vmem],
        out_specs=vmem,
        out_shape=jax.ShapeDtypeStruct((8, BLOCK + 128, RANK), bf16),
        scratch_shapes=[pltpu.VMEM((1024, RANK), bf16)],
        cost_estimate=cost(2 * 2048 * 1024 * 256, 6 << 20),
        compiler_params=room(12),
        name="partial_coeffs",
    )(where, mine, other, out_grad)


def sum_kernel(parts, out):
    total = parts[0].astype(f32)
    for i in range(1, 8):
        total += parts[i].astype(f32)
    total = total.astype(bf16)
    for i in range(8):
        out[i] = total


def sum_and_copies(parts):
    return pl.pallas_call(
        sum_kernel,
        grid=(1,),
        in_specs=[pl.BlockSpec((8, BLOCK, RANK), lambda i: (0, 0, 0))],
        out_specs=pl.BlockSpec((8, BLOCK, RANK), lambda i: (0, 0, 0)),
        out_shape=jax.ShapeDtypeStruct((8, BLOCK, RANK), bf16),
        cost_estimate=cost(8 * 65536, 2 << 20),
        compiler_params=room(8),
        name="sum_coeffs",
    )(parts)


def block_start(f):
    return jnp.minimum(ROWS * f // 16 * 16, 16 * ROWS - BLOCK)


def grad_kernel(parity, hidden, coeffs, out, rows, done):
    def load(i):
        begin = pl.multiple_of(block_start(2 * i + parity[0]), 16)
        return pltpu.make_async_copy(hidden.at[pl.ds(begin, BLOCK)], rows.at[i], done.at[i])

    for i in range(6):
        load(i).start()

    @pl.loop(0, 4)
    def _(pair):
        for j in range(2):
            load(2 * pair + j).wait()

        @pl.when(pair < 1)
        def _():
            for j in range(2):
                load(6 + j).start()

        for j in range(2):
            i = 2 * pair + j
            f = 2 * i + parity[0]
            block = jnp.dot(rows[i], coeffs[...], preferred_element_type=f32)
            block = pltpu.roll(block, BLOCK - (ROWS * f - block_start(f)), 0)
            out[i] = block[:PADDED].astype(out.dtype)


def grad_blocks(parity, hidden_t, coeffs, dtype):
    return pl.pallas_call(
        grad_kernel,
        in_specs=[
            pl.BlockSpec(memory_space=pltpu.SMEM),
            pl.BlockSpec(memory_space=pl.ANY),
            pl.BlockSpec(memory_space=pltpu.VMEM),
        ],
        out_specs=pl.BlockSpec(memory_space=pltpu.VMEM),
        out_shape=jax.ShapeDtypeStruct((8, PADDED, RANK), dtype),
        scratch_shapes=[
            pltpu.VMEM((8, BLOCK, 2048), bf16),
            pltpu.SemaphoreType.DMA((8,)),
        ],
        cost_estimate=cost(2 * 2048 * 2048 * 256, 9 << 20),
        compiler_params=room(48),
        name="grad_blocks",
    )(parity, hidden_t, coeffs)


def final_kernel(where, shares, first, second, *refs):
    pieces, (new_first, new_second, update) = refs[:10], refs[10:13]
    parts, old, new, direction, rows, blocks, came, left = refs[13:]
    column, core = where[0], where[1]

    def loads(half):
        copies = []
        for i in range(8):
            away, side = (0, 3, 1, 2)[i // 2], i % 2
            if away == 2:
                source = pieces[6 + 2 * half + side]
            else:
                source = pieces[i].at[pl.ds(4 * half, 4)]
            slot = 2 * ((column + away) % 4) + (core + side) % 2
            to = rows.at[pl.ds(4 * half, 4), slot]
            copies.append(pltpu.make_async_copy(source, to, came.at[8 * half + i]))
        return copies

    def store(i):
        begin = pl.multiple_of(1024 * i, 1024)
        return pltpu.make_async_copy(blocks.at[i], update.at[:, pl.ds(begin, 1024)], left.at[i])

    early = [
        pltpu.make_async_copy(shares, parts, came.at[16]),
        pltpu.make_async_copy(first, old.at[0], came.at[17]),
        pltpu.make_async_copy(second, old.at[1], came.at[18]),
    ]
    late = [
        pltpu.make_async_copy(new.at[0], new_first, left.at[8]),
        pltpu.make_async_copy(new.at[1], new_second, left.at[9]),
    ]
    for copy in early:
        copy.start()
    for half in range(2):
        for copy in loads(half):
            copy.start()
    for copy in early:
        copy.wait()
    grad = parts[0].astype(f32)
    for i in range(1, 8):
        grad += parts[i].astype(f32)
    grad = grad[:ROWS]
    moved = 0.9 * old[0].reshape(ROWS, RANK) + 0.1 * grad
    scale = 0.95 * old[1].reshape(ROWS, RANK) + 0.05 * grad * grad
    direction[...] = (moved / (jnp.sqrt(scale) + 1e-08)).astype(bf16)
    new[0] = moved.reshape(ROWS, 1, RANK)
    new[1] = scale.reshape(ROWS, 1, RANK)
    for copy in late:
        copy.start()
    for half in range(2):
        for copy in loads(half):
            copy.wait()

        @pl.loop(2 * half, 2 * half + 2)
        def _(pair):
            for j in range(2):
                product = lax.dot_general(
                    direction[...],
                    rows[2 * pair + j].reshape(1024, RANK),
                    (((1,), (1,)), ((), ())),
                    preferred_element_type=f32,
                )
                blocks[2 * pair + j] = (-4.0 * product).astype(bf16)
            for j in range(2):
                store(2 * pair + j).start()

    @pl.loop(0, 8)
    def _(i):
        store(i).wait()

    for copy in late:
        copy.wait()


def finish(where, shares, first, second, pieces):
    any_space = pl.BlockSpec(memory_space=pl.ANY)
    return pl.pallas_call(
        final_kernel,
        in_specs=[pl.BlockSpec(memory_space=pltpu.SMEM)] + [any_space] * 13,
        out_specs=[any_space] * 3,
        out_shape=[
            jax.ShapeDtypeStruct((ROWS, 1, RANK), f32),
            jax.ShapeDtypeStruct((ROWS, 1, RANK), f32),
            jax.ShapeDtypeStruct((ROWS, 8192), bf16),
        ],
        scratch_shapes=[
            pltpu.VMEM((8, PADDED, RANK), bf16),
            pltpu.VMEM((2, ROWS, 1, RANK), f32),
            pltpu.VMEM((2, ROWS, 1, RANK), f32),
            pltpu.VMEM((ROWS, RANK), bf16),
            pltpu.VMEM((8, 8, 128, RANK), bf16),
            pltpu.VMEM((8, ROWS, 1024), bf16),
            pltpu.SemaphoreType.DMA((19,)),
            pltpu.SemaphoreType.DMA((10,)),
        ],
        cost_estimate=cost(2 * 231 * 8192 * 256, 10 << 20),
        compiler_params=room(50),
        name="adam_update",
    )(where, shares, first, second, *pieces)


def swap_cores(value):
    return lax.ppermute(value, FSDP, [(i, i ^ 1) for i in range(16)])


def shift(value, dx, dy):
    pairs = []
    for yh in range(2):
        for x in range(4):
            for core in range(2):
                to = ((yh + dy) % 2 * 4 + (x + dx) % 4) * 2 + core
                pairs.append(((yh * 4 + x) * 2 + core, to))
    return lax.ppermute(value, FSDP, pairs)


def owners_halves(candidate, root, out_grad):
    yh, x, core = (lax.axis_index(a) for a in FSDP)
    halves = candidate.reshape(2, 512, RANK)
    kept = lax.dynamic_index_in_dim(halves, core, 0, keepdims=False)
    given = lax.dynamic_index_in_dim(halves, 1 - core, 0, keepdims=False)
    held = jnp.where(root % 2 == core, kept, swap_cores(given))
    dx = (x - root // 2 % 4) % 4
    dy = (yh - root // 8) % 2
    takes = [
        (dx == 1) & (dy == 0),
        (dx == 3) & (dy == 0),
        (dx == 0) & (dy == 1),
        dx == 2,
        (dx % 2 == 1) & (dy == 1),
    ]
    where = jnp.stack([core, x * 2 + core]).astype(jnp.int32)
    right, left, across = shift(held, 1, 0), shift(held, 3, 0), shift(held, 0, 1)
    out_grad, takes, where = lax.optimization_barrier((out_grad, takes, where))
    out_grad = hold(out_grad, 4)
    held = jnp.where(takes[0], right, jnp.where(takes[1], left, jnp.where(takes[2], across, held)))
    held, out_grad = lax.optimization_barrier((held, out_grad))
    far, across = shift(held, 2, 0), shift(held, 0, 1)
    held = jnp.where(takes[3], far, jnp.where(takes[4], across, held))
    return held, swap_cores(held), out_grad, where


def local(hidden, out_grad, projector_bank, owner, first_moment, second_moment):
    core = lax.axis_index("core")
    column = lax.axis_index("x")

    mine, other, held_grad, where = owners_halves(projector_bank[0], owner[0], out_grad)
    outgoing = partial_and_share(where, mine, other, held_grad)
    parts = lax.all_to_all(outgoing, TP, 0, 0)
    share = parts[:, BLOCK:]
    coeffs = lax.all_to_all(sum_and_copies(parts), TP, 0, 0).reshape(2048, RANK)

    hidden_t = hidden.T
    give = grad_blocks((1 - core)[None], hidden_t, coeffs, bf16)
    give, left, right = lax.optimization_barrier((give, shift(share, 1, 0), shift(share, 3, 0)))
    ring = [share, left, right, shift(left[:4], 1, 0), shift(right[4:], 3, 0)]
    got = swap_cores(give)
    keep = grad_blocks(core[None], hidden_t, coeffs, f32)
    pair = (keep + got.astype(f32)).astype(bf16)
    pair, *ring = lax.optimization_barrier((pair, *ring))
    shares = lax.all_to_all(pair, CHIPS, 0, 0)
    pieces = [side for piece in ring for side in (piece, swap_cores(piece))]
    new_first, new_second, update = finish(
        jnp.stack([column, core]).astype(jnp.int32),
        shares,
        first_moment.transpose(1, 0, 2),
        second_moment.transpose(1, 0, 2),
        pieces,
    )
    return (new_first.transpose(1, 0, 2), new_second.transpose(1, 0, 2), update[None])


def solution(mesh):
    fine = jax.sharding.Mesh(
        mesh.devices.reshape(2, 4, 2, 4, 2), ("yh", "x", "core", "z", "yl")
    )
    in_specs = (
        P(FSDP, TP),
        P(FSDP, TP),
        P(FSDP, TP, None),
        P(),
        P(TP, FSDP, None),
        P(TP, FSDP, None),
    )
    out_specs = (P(TP, FSDP, None), P(TP, FSDP, None), P(TP, FSDP, None))
    return jax.shard_map(local, mesh=fine, in_specs=in_specs, out_specs=out_specs, check_vma=False)
```

```python
import functools

import jax
import jax.numpy as jnp
from jax import lax
from jax.experimental import pallas as pl
from jax.experimental.pallas import tpu as pltpu
from jax.sharding import PartitionSpec as P

FSDP = ("yh", "x", "core")
CHIPS = ("yh", "x")
TP = ("z", "yl")
ROWS = 231
PADDED = 232
BLOCK = 256
RANK = 256
bf16, f32 = jnp.bfloat16, jnp.float32


def cost(flops, moved):
    return pl.CostEstimate(flops=flops, bytes_accessed=moved, transcendentals=0)


def room(mebibytes):
    return pltpu.CompilerParams(vmem_limit_bytes=mebibytes << 20)


def hold_kernel(count, source, out, done):
    rows = source.shape[0] // count
    copies = [
        pltpu.make_async_copy(
            source.at[pl.ds(rows * i, rows)], out.at[pl.ds(rows * i, rows)], done.at[i]
        )
        for i in range(count)
    ]
    for copy in copies:
        copy.start()
    for copy in copies:
        copy.wait()


def hold(source, count):
    return pl.pallas_call(
        functools.partial(hold_kernel, count),
        in_specs=[pl.BlockSpec(memory_space=pl.ANY)],
        out_specs=pl.BlockSpec(memory_space=pltpu.VMEM),
        out_shape=jax.ShapeDtypeStruct(source.shape, source.dtype),
        scratch_shapes=[pltpu.SemaphoreType.DMA((count,))],
        cost_estimate=cost(0, 4 * source.size),
        compiler_params=room(4),
        name="hold",
    )(source)


def partial_kernel(where, mine, other, grad, out, piece):
    core, half = where[0], mine.shape[0]
    piece[pl.ds(pl.multiple_of(core * half, half), half), :] = mine[...]
    piece[pl.ds(pl.multiple_of((1 - core) * half, half), half), :] = other[...]

    below = piece[pl.ds(pl.multiple_of(where[1] * 128, 128), 128), :]
    for i in range(8):
        out[i, BLOCK:, :] = below

    @pl.loop(0, 2)
    def _(pair):
        for j in range(2):
            i = 2 * pair + j
            rows = grad[pl.ds(pl.multiple_of(512 * i, 512), 512), :]
            product = jnp.dot(rows, piece[...], preferred_element_type=f32).astype(bf16)
            out[2 * i, :BLOCK, :] = product[:BLOCK]
            out[2 * i + 1, :BLOCK, :] = product[BLOCK:]


def partial_and_share(where, mine, other, out_grad):
    vmem = pl.BlockSpec(memory_space=pltpu.VMEM)
    return pl.pallas_call(
        partial_kernel,
        in_specs=[pl.BlockSpec(memory_space=pltpu.SMEM), vmem, vmem, vmem],
        out_specs=vmem,
        out_shape=jax.ShapeDtypeStruct((8, BLOCK + 128, RANK), bf16),
        scratch_shapes=[pltpu.VMEM((1024, RANK), bf16)],
        cost_estimate=cost(2 * 2048 * 1024 * 256, 6 << 20),
        compiler_params=room(12),
        name="partial_coeffs",
    )(where, mine, other, out_grad)


def sum_kernel(parts, out):
    total = parts[0].astype(f32)
    for i in range(1, 8):
        total += parts[i].astype(f32)
    total = total.astype(bf16)
    for i in range(8):
        out[i] = total


def sum_and_copies(parts):
    return pl.pallas_call(
        sum_kernel,
        grid=(1,),
        in_specs=[pl.BlockSpec((8, BLOCK, RANK), lambda i: (0, 0, 0))],
        out_specs=pl.BlockSpec((8, BLOCK, RANK), lambda i: (0, 0, 0)),
        out_shape=jax.ShapeDtypeStruct((8, BLOCK, RANK), bf16),
        cost_estimate=cost(8 * 65536, 2 << 20),
        compiler_params=room(8),
        name="sum_coeffs",
    )(parts)


def block_start(f):
    return jnp.minimum(ROWS * f // 16 * 16, 16 * ROWS - BLOCK)


def grad_kernel(parity, hidden, coeffs, out, rows, done):
    def load(i):
        begin = pl.multiple_of(block_start(2 * i + parity[0]), 16)
        return pltpu.make_async_copy(hidden.at[pl.ds(begin, BLOCK)], rows.at[i], done.at[i])

    for i in range(6):
        load(i).start()

    @pl.loop(0, 4)
    def _(pair):
        for j in range(2):
            load(2 * pair + j).wait()

        @pl.when(pair < 1)
        def _():
            for j in range(2):
                load(6 + j).start()

        for j in range(2):
            i = 2 * pair + j
            f = 2 * i + parity[0]
            block = jnp.dot(rows[i], coeffs[...], preferred_element_type=f32)
            block = pltpu.roll(block, BLOCK - (ROWS * f - block_start(f)), 0)
            out[i] = block[:PADDED].astype(out.dtype)


def grad_blocks(parity, hidden_t, coeffs, dtype):
    return pl.pallas_call(
        grad_kernel,
        in_specs=[
            pl.BlockSpec(memory_space=pltpu.SMEM),
            pl.BlockSpec(memory_space=pl.ANY),
            pl.BlockSpec(memory_space=pltpu.VMEM),
        ],
        out_specs=pl.BlockSpec(memory_space=pltpu.VMEM),
        out_shape=jax.ShapeDtypeStruct((8, PADDED, RANK), dtype),
        scratch_shapes=[
            pltpu.VMEM((8, BLOCK, 2048), bf16),
            pltpu.SemaphoreType.DMA((8,)),
        ],
        cost_estimate=cost(2 * 2048 * 2048 * 256, 9 << 20),
        compiler_params=room(48),
        name="grad_blocks",
    )(parity, hidden_t, coeffs)


def final_kernel(where, shares, first, second, *refs):
    pieces, (new_first, new_second, update) = refs[:10], refs[10:13]
    parts, old, new, direction, rows, blocks, came, left = refs[13:]
    column, core = where[0], where[1]

    def loads(half):
        copies = []
        for i in range(8):
            away, side = (0, 3, 1, 2)[i // 2], i % 2
            if away == 2:
                source = pieces[6 + 2 * half + side]
            else:
                source = pieces[i].at[pl.ds(4 * half, 4)]
            slot = 2 * ((column + away) % 4) + (core + side) % 2
            to = rows.at[pl.ds(4 * half, 4), slot]
            copies.append(pltpu.make_async_copy(source, to, came.at[8 * half + i]))
        return copies

    def store(i):
        begin = pl.multiple_of(1024 * i, 1024)
        return pltpu.make_async_copy(blocks.at[i], update.at[:, pl.ds(begin, 1024)], left.at[i])

    early = [
        pltpu.make_async_copy(shares, parts, came.at[16]),
        pltpu.make_async_copy(first, old.at[0], came.at[17]),
        pltpu.make_async_copy(second, old.at[1], came.at[18]),
    ]
    late = [
        pltpu.make_async_copy(new.at[0], new_first, left.at[8]),
        pltpu.make_async_copy(new.at[1], new_second, left.at[9]),
    ]
    for copy in early:
        copy.start()
    for half in range(2):
        for copy in loads(half):
            copy.start()
    for copy in early:
        copy.wait()
    grad = parts[0].astype(f32)
    for i in range(1, 8):
        grad += parts[i].astype(f32)
    grad = grad[:ROWS]
    moved = 0.9 * old[0].reshape(ROWS, RANK) + 0.1 * grad
    scale = 0.95 * old[1].reshape(ROWS, RANK) + 0.05 * grad * grad
    direction[...] = (moved / (jnp.sqrt(scale) + 1e-08)).astype(bf16)
    new[0] = moved.reshape(ROWS, 1, RANK)
    new[1] = scale.reshape(ROWS, 1, RANK)
    for copy in late:
        copy.start()
    for half in range(2):
        for copy in loads(half):
            copy.wait()

        @pl.loop(2 * half, 2 * half + 2)
        def _(pair):
            for j in range(2):
                product = lax.dot_general(
                    direction[...],
                    rows[2 * pair + j].reshape(1024, RANK),
                    (((1,), (1,)), ((), ())),
                    preferred_element_type=f32,
                )
                blocks[2 * pair + j] = (-4.0 * product).astype(bf16)
            for j in range(2):
                store(2 * pair + j).start()

    @pl.loop(0, 8)
    def _(i):
        store(i).wait()

    for copy in late:
        copy.wait()


def finish(where, shares, first, second, pieces):
    any_space = pl.BlockSpec(memory_space=pl.ANY)
    return pl.pallas_call(
        final_kernel,
        in_specs=[pl.BlockSpec(memory_space=pltpu.SMEM)] + [any_space] * 13,
        out_specs=[any_space] * 3,
        out_shape=[
            jax.ShapeDtypeStruct((ROWS, 1, RANK), f32),
            jax.ShapeDtypeStruct((ROWS, 1, RANK), f32),
            jax.ShapeDtypeStruct((ROWS, 8192), bf16),
        ],
        scratch_shapes=[
            pltpu.VMEM((8, PADDED, RANK), bf16),
            pltpu.VMEM((2, ROWS, 1, RANK), f32),
            pltpu.VMEM((2, ROWS, 1, RANK), f32),
            pltpu.VMEM((ROWS, RANK), bf16),
            pltpu.VMEM((8, 8, 128, RANK), bf16),
            pltpu.VMEM((8, ROWS, 1024), bf16),
            pltpu.SemaphoreType.DMA((19,)),
            pltpu.SemaphoreType.DMA((10,)),
        ],
        cost_estimate=cost(2 * 231 * 8192 * 256, 10 << 20),
        compiler_params=room(50),
        name="adam_update",
    )(where, shares, first, second, *pieces)


def swap_cores(value):
    return lax.ppermute(value, FSDP, [(i, i ^ 1) for i in range(16)])


def shift(value, dx, dy):
    pairs = []
    for yh in range(2):
        for x in range(4):
            for core in range(2):
                to = ((yh + dy) % 2 * 4 + (x + dx) % 4) * 2 + core
                pairs.append(((yh * 4 + x) * 2 + core, to))
    return lax.ppermute(value, FSDP, pairs)


def owners_halves(candidate, root, out_grad):
    yh, x, core = (lax.axis_index(a) for a in FSDP)
    halves = candidate.reshape(2, 512, RANK)
    kept = lax.dynamic_index_in_dim(halves, core, 0, keepdims=False)
    given = lax.dynamic_index_in_dim(halves, 1 - core, 0, keepdims=False)
    held = jnp.where(root % 2 == core, kept, swap_cores(given))
    dx = (x - root // 2 % 4) % 4
    dy = (yh - root // 8) % 2
    takes = [
        (dx == 1) & (dy == 0),
        (dx == 3) & (dy == 0),
        (dx == 0) & (dy == 1),
        dx == 2,
        (dx % 2 == 1) & (dy == 1),
    ]
    where = jnp.stack([core, x * 2 + core]).astype(jnp.int32)
    right, left, across = shift(held, 1, 0), shift(held, 3, 0), shift(held, 0, 1)
    out_grad, takes, where = lax.optimization_barrier((out_grad, takes, where))
    out_grad = hold(out_grad, 4)
    held = jnp.where(takes[0], right, jnp.where(takes[1], left, jnp.where(takes[2], across, held)))
    held, out_grad = lax.optimization_barrier((held, out_grad))
    far, across = shift(held, 2, 0), shift(held, 0, 1)
    held = jnp.where(takes[3], far, jnp.where(takes[4], across, held))
    return held, swap_cores(held), out_grad, where


def local(hidden, out_grad, projector_bank, owner, first_moment, second_moment):
    core = lax.axis_index("core")
    column = lax.axis_index("x")

    mine, other, held_grad, where = owners_halves(projector_bank[0], owner[0], out_grad)
    outgoing = partial_and_share(where, mine, other, held_grad)
    parts = lax.all_to_all(outgoing, TP, 0, 0)
    share = parts[:, BLOCK:]
    coeffs = lax.all_to_all(sum_and_copies(parts), TP, 0, 0).reshape(2048, RANK)

    hidden_t = hidden.T
    give = grad_blocks((1 - core)[None], hidden_t, coeffs, bf16)
    give, left, right = lax.optimization_barrier((give, shift(share, 1, 0), shift(share, 3, 0)))
    ring = [share, left, right, shift(left[:4], 1, 0), shift(right[4:], 3, 0)]
    got = swap_cores(give)
    keep = grad_blocks(core[None], hidden_t, coeffs, f32)
    pair = (keep + got.astype(f32)).astype(bf16)
    pair, *ring = lax.optimization_barrier((pair, *ring))
    shares = lax.all_to_all(pair, CHIPS, 0, 0)
    pieces = [side for piece in ring for side in (piece, swap_cores(piece))]
    new_first, new_second, update = finish(
        jnp.stack([column, core]).astype(jnp.int32),
        shares,
        first_moment.transpose(1, 0, 2),
        second_moment.transpose(1, 0, 2),
        pieces,
    )
    return (new_first.transpose(1, 0, 2), new_second.transpose(1, 0, 2), update[None])


def solution(mesh):
    fine = jax.sharding.Mesh(
        mesh.devices.reshape(2, 4, 2, 4, 2), ("yh", "x", "core", "z", "yl")
    )
    in_specs = (
        P(FSDP, TP),
        P(FSDP, TP),
        P(FSDP, TP, None),
        P(),
        P(TP, FSDP, None),
        P(TP, FSDP, None),
    )
    out_specs = (P(TP, FSDP, None), P(TP, FSDP, None), P(TP, FSDP, None))
    return jax.shard_map(local, mesh=fine, in_specs=in_specs, out_specs=out_specs, check_vma=False)
```
